32 devices in a mesh: seq: 16 (over z, y, x), tp: 2 (over core).
Axes of the slice: x: 2, y: 2, z: 4, core: 2. Of those that a mesh axis runs over, the one named last changes fastest.
Arguments:
- query: bfloat16 [128, 2048], P('seq', 'tp'), may hold values from -8 to 8, as said below
- new_key: bfloat16 [128, 2048], P('seq', 'tp'), may hold values from -6 to 6
- new_value: bfloat16 [128, 2048], P('seq', 'tp'), may hold values from -6 to 6
- key_pool: bfloat16 [640, 64, 2048], P('seq', None, 'tp'), may hold values from -6 to 6
- value_pool: bfloat16 [640, 64, 2048], P('seq', None, 'tp'), may hold values from -6 to 6
- long_key: bfloat16 [4, 4096, 2048], P(None, 'seq', 'tp'), may hold values from -6 to 6
- long_value: bfloat16 [4, 4096, 2048], P(None, 'seq', 'tp'), may hold values from -6 to 6
- serve_table: int32 [160], P('seq'), may hold values from -1 to 127, as said below
- serve_len: int32 [160], P('seq'), may hold values from 0 to 256, as said below
- page_slot: int32 [640], P('seq'), may hold values from -1 to 9, as said below
- page_offset: int32 [640], P('seq'), may hold values from 0 to 192, as said below
- long_request: int32 [4], replicated, may hold values from 7 to 127, as said below
- long_len: int32 [4], replicated, may hold values from 2048 to 4096
- lambda_head: float32 [8], P('tp'), may hold values from 0.2 to 0.8
- norm_gain: float32 [2048], P('tp'), may hold values from 0.5 to 1.5
- out_weight: bfloat16 [2048, 2048], P('tp'), may hold values from -0.125 to 0.125
Outputs:
- layer_out: bfloat16 [128, 2048], P('seq', 'tp')
The draws below stay inside these ranges and needn't reach their ends.
Inputs may be any that keep to these rules, and one draw needn't show every extreme that they name: `query`: rows r with r % 4 == 0 or r % 8 == 7 and all others follow the table's range. `serve_table`: every request that is not a long request stands in exactly one slot, possibly of another index of seq than its own; long requests stand in none; some index of seq fills all 10 slots. `serve_len`: the length of a request that stands in a slot is 1 or more. `page_slot`: A slot of length L owns exactly ceil(L / 64) pages of its own index of seq, with offsets 0, 64, 128 and so on; some index of seq uses all 40 pages. `page_offset`: free pages have offset 0. `long_request`: distinct request numbers.
All inputs are finite; a program needn't handle non-finite values.
Results may differ from the reference program's by a relative error of at most 0.019.
Values may be sent and summed in bfloat16 or wider, within the bound.
A program may use at most 64 MiB of HBM per device.

```python
import jax
import jax.numpy as jnp
from jax import lax

D = 2048
HEADS = 8
DH = 128
DV = 256
REQ_DEV = 8
PG = 64
MAXP = 4
NLONG = 4
LLEN_DEV = 256
SERVE = 10
PAGES_DEV = 40
REQS = 128
POOL = 640
LLEN = 4096
N_SEQ = 16


def layout(key):
    layout_key = jax.random.fold_in(key, 7001)
    n_devices = REQS // REQ_DEV
    stride = n_devices // NLONG
    long_index = jnp.arange(NLONG)
    jitter = jax.random.randint(jax.random.fold_in(layout_key, 10), (NLONG,), 0, max(stride // 2, 1))
    jitter = jnp.where((long_index == 0) | (long_index == NLONG - 1), 0, jitter)
    long_dev = jnp.where(long_index == NLONG - 1, 0, n_devices - 1 - long_index * stride - 2 * jitter)
    start_dev = n_devices - 2 - jax.random.randint(jax.random.fold_in(layout_key, 1), (), 0, NLONG - 1) * stride
    offset_dev = jax.random.randint(jax.random.fold_in(layout_key, 2), (), 1, n_devices)
    devices = jnp.arange(n_devices)
    leaving = jax.random.randint(jax.random.fold_in(layout_key, 3), (n_devices,), 0, 3)
    sender = (start_dev - offset_dev) % n_devices
    leaving = jnp.where(devices == start_dev, 0, leaving)
    leaving = jnp.where(devices == sender, 2, leaving)
    long_ids = long_dev * REQ_DEV + REQ_DEV - 1
    is_long_dev = jnp.any(devices[:, None] == long_dev[None, :], axis=1)
    requests = jnp.arange(REQS)
    home_dev = requests // REQ_DEV
    local_idx = requests % REQ_DEV
    lengths = jax.random.randint(jax.random.fold_in(layout_key, 4), (REQS,), PG // 2, MAXP * PG + 1)
    full_len = jax.random.randint(jax.random.fold_in(layout_key, 5), (REQS,), (MAXP - 1) * PG + 1, MAXP * PG + 1)
    forced = (home_dev == start_dev) | (home_dev == sender) & (local_idx < 2)
    lengths = jnp.where(forced, full_len, lengths)
    lengths = jnp.where(requests == start_dev * REQ_DEV, MAXP * PG, lengths)
    own_slots = jnp.arange(REQ_DEV)
    own_ids = devices[:, None] * REQ_DEV + own_slots[None, :]
    own_ok = (own_slots[None, :] >= leaving[:, None]) & jnp.logical_not((own_slots[None, :] == REQ_DEV - 1) & is_long_dev[:, None])
    source = (devices - offset_dev) % n_devices
    in_slots = jnp.arange(2)
    in_ids = source[:, None] * REQ_DEV + in_slots[None, :]
    in_ok = in_slots[None, :] < leaving[source][:, None]
    serve_ids = jnp.concatenate([jnp.where(own_ok, own_ids, -1), jnp.where(in_ok, in_ids, -1)], axis=1)
    slot_len = jnp.where(serve_ids >= 0, lengths[jnp.maximum(serve_ids, 0)], 0)
    counts = (slot_len + PG - 1) // PG
    first_page = jnp.cumsum(counts, axis=1) - counts
    page_ids = jnp.arange(PAGES_DEV)
    inside = (page_ids[None, None, :] >= first_page[:, :, None]) & (page_ids[None, None, :] < (first_page + counts)[:, :, None])
    slot_of = jnp.sum(jnp.where(inside, jnp.arange(SERVE)[None, :, None] + 1, 0), axis=1) - 1
    page_off = jnp.sum(jnp.where(inside, (page_ids[None, None, :] - first_page[:, :, None]) * PG, 0), axis=1)
    perm_key = jax.random.fold_in(layout_key, 6)
    orders = jax.vmap(lambda device: jax.random.permutation(jax.random.fold_in(perm_key, device), PAGES_DEV))(devices)
    slot_of = jnp.take_along_axis(slot_of, orders, axis=1)
    page_off = jnp.take_along_axis(page_off, orders, axis=1)
    long_order = jax.random.permutation(jax.random.fold_in(layout_key, 11), NLONG)
    long_ids = long_ids[long_order]
    longest = jax.random.randint(jax.random.fold_in(layout_key, 8), (), 0, NLONG)
    long_lengths = jax.random.randint(jax.random.fold_in(layout_key, 9), (NLONG,), LLEN // 2, LLEN + 1)
    long_lengths = jnp.where(jnp.arange(NLONG) == longest, LLEN, long_lengths)
    return (serve_ids, slot_len, slot_of, page_off, long_ids, long_lengths)


def draw_serve_table(key, part):
    return layout(key)[0].reshape(-1).astype(jnp.int32)


def draw_serve_len(key, part):
    return layout(key)[1].reshape(-1).astype(jnp.int32)


def draw_page_slot(key, part):
    return layout(key)[2].reshape(-1).astype(jnp.int32)


def draw_page_offset(key, part):
    return layout(key)[3].reshape(-1).astype(jnp.int32)


def draw_long_request(key, part):
    return layout(key)[4].astype(jnp.int32)


def draw_long_len(key, part):
    return layout(key)[5].astype(jnp.int32)


def draw_query(key, part):
    shape = (REQS, HEADS * 2 * DH)
    values = jnp.clip(jax.random.normal(jax.random.fold_in(key, 9201), shape, jnp.float32), -6.0, 6.0)
    return values.astype(jnp.bfloat16)


def draw_key_pool(key, part):
    shape = (POOL, PG, HEADS * 2 * DH)
    values = jnp.clip(jax.random.normal(jax.random.fold_in(key, 9301), shape, jnp.float32), -6.0, 6.0)
    return values.astype(jnp.bfloat16)


def draw_long_key(key, part):
    shape = (NLONG, LLEN, HEADS * 2 * DH)
    values = jnp.clip(jax.random.normal(jax.random.fold_in(key, 9401), shape, jnp.float32), -6.0, 6.0)
    return values.astype(jnp.bfloat16)


def steps_of(rng, shape, split, low, top_value):
    level, own = 1.0, jax.random.fold_in(rng, 6)
    for axis_at, shards_of in split:
        steps = jnp.exp(jax.random.uniform(jax.random.fold_in(own, axis_at), (shards_of,), jnp.float32, low / len(split), top_value / len(split)))
        level = level * jnp.repeat(steps, shape[axis_at] // shards_of).reshape([-1 if axis == axis_at else 1 for axis in range(len(shape))])
    return level


def gaussian(stream_key, shape, scale, reach, cuts=(), kind=jnp.bfloat16):
    values = scale * jax.random.normal(stream_key, shape, jnp.float32)
    if cuts:
        values = values * steps_of(stream_key, shape, cuts, -0.22, 0.18)
    return jnp.clip(values, -reach, reach).astype(kind)


def setup_inputs(seed: int = 0) -> dict:
    key_of = jax.random.split(jax.random.key(seed), 17)
    return {
        "query": draw_query(jax.random.fold_in(key_of[16], 71), 0),
        "new_key": gaussian(key_of[1], (REQS, HEADS * 2 * DH), 1.0, 6.0, ((0, 16), (1, 2))),
        "new_value": gaussian(key_of[2], (REQS, HEADS * DV), 1.0, 6.0, ((0, 16), (1, 2))),
        "key_pool": draw_key_pool(jax.random.fold_in(key_of[16], 71), 0),
        "value_pool": gaussian(key_of[4], (POOL, PG, HEADS * DV), 1.0, 6.0, ((0, 16), (2, 2))),
        "long_key": draw_long_key(jax.random.fold_in(key_of[16], 71), 0),
        "long_value": gaussian(key_of[6], (NLONG, LLEN, HEADS * DV), 1.0, 6.0, ((1, 16), (2, 2))),
        "serve_table": draw_serve_table(jax.random.fold_in(key_of[16], 71), 0),
        "serve_len": draw_serve_len(jax.random.fold_in(key_of[16], 71), 0),
        "page_slot": draw_page_slot(jax.random.fold_in(key_of[16], 71), 0),
        "page_offset": draw_page_offset(jax.random.fold_in(key_of[16], 71), 0),
        "long_request": draw_long_request(jax.random.fold_in(key_of[16], 71), 0),
        "long_len": draw_long_len(jax.random.fold_in(key_of[16], 71), 0),
        "lambda_head": jnp.clip(0.2 + 0.6 * jax.random.uniform(key_of[13], (HEADS,), jnp.float32) ** steps_of(key_of[13], (HEADS,), ((0, 2),), -0.2, 0.2), 0.2, 0.8),
        "norm_gain": jnp.clip(1.0 + 0.1 * jax.random.normal(key_of[14], (HEADS * DV,), jnp.float32), 0.5, 1.5),
        "out_weight": gaussian(key_of[15], (HEADS * DV, D), (HEADS * DV) ** -0.5, 0.125, ((0, 2),)),
    }


MASKED = -1e+30

def page_terms(keys, values, page_q, live):
    page_count = keys.shape[0]
    cell_count = keys.shape[1]
    head_count = page_q.shape[1]
    shaped_keys = keys.astype(jnp.float32).reshape(page_count, cell_count, head_count, 2, DH)
    scores = jnp.einsum('pchjd,phjd->pchj', shaped_keys, page_q.astype(jnp.float32), precision=lax.Precision.HIGHEST) * DH ** (-0.5)
    live_mask = live[:, :, None, None]
    scores = jnp.where(live_mask, scores, MASKED)
    page_max = lax.optimization_barrier(jnp.max(scores, axis=1))
    weights = jnp.where(live_mask, jnp.exp(scores - page_max[:, None]), 0.0)
    page_sum = lax.optimization_barrier(jnp.sum(weights, axis=1))
    rounded = lax.optimization_barrier(weights.astype(jnp.bfloat16)).astype(jnp.float32)
    shaped_values = values.astype(jnp.float32).reshape(page_count, cell_count, head_count, DV)
    page_num = jnp.einsum('pchj,pchv->phjv', rounded, shaped_values, precision=lax.Precision.HIGHEST)
    return (page_max, page_sum, page_num)

def block_terms(operands):
    return page_terms(operands[0], operands[1], operands[2], operands[3])

def reference(query, new_key, new_value, key_pool, value_pool, long_key, long_value, serve_table, serve_len, page_slot, page_offset, long_request, long_len, lambda_head, norm_gain, out_weight):
    queries = query.reshape(REQS, HEADS, 2, DH)
    device_of = jnp.arange(POOL, dtype=jnp.int32) // PAGES_DEV
    slot_index = (device_of * SERVE + jnp.maximum(page_slot, 0)).astype(jnp.int32)
    page_req = jnp.where(page_slot >= 0, serve_table[slot_index], -1)
    page_len = jnp.where(page_slot >= 0, serve_len[slot_index], 0)
    page_q = queries[jnp.maximum(page_req, 0)]
    cell_pos = page_offset[:, None] + jnp.arange(PG, dtype=jnp.int32)[None, :]
    live = (page_slot[:, None] >= 0) & (cell_pos < page_len[:, None])
    pool_max, pool_sum, pool_num = lax.map(block_terms, (key_pool.reshape(N_SEQ, PAGES_DEV, PG, HEADS * 2 * DH), value_pool.reshape(N_SEQ, PAGES_DEV, PG, HEADS * DV), page_q.reshape(N_SEQ, PAGES_DEV, HEADS, 2, DH), live.reshape(N_SEQ, PAGES_DEV, PG)))
    pool_max = pool_max.reshape(POOL, HEADS, 2)
    pool_sum = pool_sum.reshape(POOL, HEADS, 2)
    pool_num = pool_num.reshape(POOL, HEADS, 2, DV)
    per_long = LLEN // PG
    long_pages = NLONG * per_long
    long_q = jnp.repeat(queries[long_request], per_long, axis=0)
    long_pos = jnp.arange(LLEN, dtype=jnp.int32).reshape(per_long, PG)
    long_live = (long_pos[None] < long_len[:, None, None]).reshape(long_pages, PG)
    block_pages = LLEN_DEV // PG
    long_max, long_sum, long_num = lax.map(block_terms, (long_key.reshape(NLONG * N_SEQ, block_pages, PG, HEADS * 2 * DH), long_value.reshape(NLONG * N_SEQ, block_pages, PG, HEADS * DV), long_q.reshape(NLONG * N_SEQ, block_pages, HEADS, 2, DH), long_live.reshape(NLONG * N_SEQ, block_pages, PG)))
    every_max = jnp.concatenate([pool_max, long_max.reshape(long_pages, HEADS, 2)], axis=0)
    every_sum = jnp.concatenate([pool_sum, long_sum.reshape(long_pages, HEADS, 2)], axis=0)
    every_num = jnp.concatenate([pool_num, long_num.reshape(long_pages, HEADS, 2, DV)], axis=0)
    owner_ids = jnp.concatenate([page_req, jnp.repeat(long_request, per_long)], axis=0).astype(jnp.int32)
    segment = jnp.where(owner_ids >= 0, owner_ids, REQS).astype(jnp.int32)
    own_scores = jnp.einsum('rhjd,rhjd->rhj', queries.astype(jnp.float32), new_key.reshape(REQS, HEADS, 2, DH).astype(jnp.float32), precision=lax.Precision.HIGHEST) * DH ** (-0.5)
    seg_max = jax.ops.segment_max(every_max, segment, num_segments=REQS + 1)[:REQS]
    best = jnp.maximum(own_scores, seg_max)
    best_ext = jnp.concatenate([best, jnp.zeros((1, HEADS, 2), jnp.float32)], axis=0)
    valid = (owner_ids >= 0)[:, None, None]
    factor = jnp.where(valid, jnp.exp(jnp.where(valid, every_max - best_ext[segment], 0.0)), 0.0)
    own_weight = jnp.exp(own_scores - best)
    denom = own_weight + jax.ops.segment_sum(factor * every_sum, segment, num_segments=REQS + 1)[:REQS]
    numer = own_weight[..., None] * new_value.reshape(REQS, HEADS, 1, DV).astype(jnp.float32)
    numer = numer + jax.ops.segment_sum(factor[..., None] * every_num, segment, num_segments=REQS + 1)[:REQS]
    attn = numer / denom[..., None]
    diff = attn[:, :, 0] - lambda_head[None, :, None] * attn[:, :, 1]
    normed = diff * lax.rsqrt(lax.optimization_barrier(jnp.mean(diff * diff, axis=-1, keepdims=True)) + 1e-05) * norm_gain.reshape(HEADS, DV)
    normed = normed.astype(jnp.bfloat16).reshape(REQS, HEADS * DV)
    return jnp.dot(normed, out_weight, preferred_element_type=jnp.float32).astype(jnp.bfloat16)
```

```python
import functools

import jax
import jax.numpy as jnp
from jax import lax
from jax.experimental import pallas as pl
from jax.experimental.pallas import tpu as pltpu
from jax.sharding import PartitionSpec as P

DH = 128
DV = 256
PG = 64
LANES = 128
ROWS = 16
MASKED = -1e30
MESH = pl.DeviceIdType.MESH


def split3(x):
    high = x.astype(jnp.bfloat16).astype(jnp.float32)
    rest = x - high
    mid = rest.astype(jnp.bfloat16).astype(jnp.float32)
    return high, mid, rest - mid


def lane_pack(lane, columns):
    packed = jnp.zeros(lane.shape, jnp.float32)
    for at, column in enumerate(columns):
        packed = jnp.where(lane == at, column, packed)
    return packed


def kernel(
    seq_count,
    tp_count,
    heads,
    table_ref,
    len_ref,
    slot_ref,
    offset_ref,
    long_request_ref,
    long_len_ref,
    lambda_ref,
    query_ref,
    new_key_ref,
    new_value_ref,
    gain_ref,
    key_ref,
    value_ref,
    long_key_ref,
    long_value_ref,
    weight_ref,
    out_ref,
    key_buf,
    value_buf,
    long_key_buf,
    long_value_buf,
    weight_buf,
    bias_buf,
    own_query,
    all_query,
    term_out,
    term_in,
    attn_out,
    attn_in,
    part_out,
    part_in,
    load_sem,
    query_send,
    query_recv,
    term_send,
    term_recv,
    attn_send,
    attn_recv,
    part_send,
    part_recv,
):
    me = lax.axis_index("seq")
    tp_me = lax.axis_index("tp")
    blocks = heads * 2 * DV // LANES
    groups = seq_count // blocks
    group = me // blocks
    block_me = me % blocks
    req_count = query_ref.shape[0]
    serve_count = table_ref.shape[0]
    page_count = slot_ref.shape[0]
    long_count = long_request_ref.shape[0]
    long_cells = long_key_ref.shape[1]
    pool_cells = page_count * PG
    out_cols = weight_ref.shape[1] // tp_count

    loads = []
    for h in range(heads):
        cols = pl.ds(h * 2 * DH, 2 * DH)
        row = []
        for at, (src, dst) in enumerate(
            (
                (key_ref, key_buf),
                (long_key_ref, long_key_buf),
                (value_ref, value_buf),
                (long_value_ref, long_value_buf),
            )
        ):
            row.append(
                pltpu.make_async_copy(src.at[:, :, cols], dst.at[h], load_sem.at[4 * h + at])
            )
        loads.append(row)
    weight_load = pltpu.make_async_copy(weight_ref, weight_buf, load_sem.at[4 * heads])

    barrier = pltpu.get_barrier_semaphore()
    for k in range(1, seq_count):
        pl.semaphore_signal(
            barrier, inc=1, device_id={"seq": lax.rem(me + k, seq_count)}, device_id_type=MESH
        )
    for k in range(1, tp_count):
        pl.semaphore_signal(
            barrier, inc=1, device_id={"tp": lax.rem(tp_me + k, tp_count)}, device_id_type=MESH
        )
    for row in loads:
        for copy in row:
            copy.start()
    weight_load.start()

    query = query_ref[...].astype(jnp.float32)
    half = query.shape[1] // 2
    own_query[...] = jnp.concatenate([query[:, :half], query[:, half:]], axis=0).astype(
        jnp.bfloat16
    )
    all_query[me] = own_query[...]
    pl.semaphore_wait(barrier, seq_count + tp_count - 2)

    def query_copy(target, owner, at):
        return pltpu.make_async_remote_copy(
            src_ref=own_query,
            dst_ref=all_query.at[owner],
            send_sem=query_send.at[at],
            recv_sem=query_recv.at[owner],
            device_id={"seq": target},
            device_id_type=MESH,
        )

    for k in range(1, seq_count):
        query_copy(lax.rem(me + k, seq_count), me, k - 1).start()

    lane = lax.broadcasted_iota(jnp.int32, (ROWS, LANES), 1)
    slot_row = lax.broadcasted_iota(jnp.int32, (ROWS, LANES), 0)
    length = jnp.zeros((ROWS, LANES), jnp.int32)
    owner = jnp.full((ROWS, LANES), -1, jnp.int32)
    for s in range(serve_count):
        length = jnp.where(slot_row == s, len_ref[s], length)
        owner = jnp.where(slot_row == s, table_ref[s], owner)
    for n in range(long_count):
        owner = jnp.where(slot_row == serve_count + n, long_request_ref[n], owner)
    per_chunk = LANES // PG
    for chunk in range(pool_cells // LANES):
        slot = jnp.full((ROWS, LANES), slot_ref[chunk * per_chunk], jnp.int32)
        offset = jnp.full((ROWS, LANES), offset_ref[chunk * per_chunk], jnp.int32)
        for extra in range(1, per_chunk):
            beyond = lane >= extra * PG
            slot = jnp.where(beyond, slot_ref[chunk * per_chunk + extra], slot)
            offset = jnp.where(beyond, offset_ref[chunk * per_chunk + extra], offset)
        live = (slot == slot_row) & (offset + (lane & (PG - 1)) < length)
        bias_buf[:, chunk * LANES : (chunk + 1) * LANES] = jnp.where(live, 0.0, MASKED)
    for n in range(long_count):
        for chunk in range(long_cells // LANES):
            pos = me * long_cells + chunk * LANES + lane
            live = (slot_row == serve_count + n) & (pos < long_len_ref[n])
            start = pool_cells + n * long_cells + chunk * LANES
            bias_buf[:, start : start + LANES] = jnp.where(live, 0.0, MASKED)

    products = query * new_key_ref[...].astype(jnp.float32)
    own_scores = [
        jnp.sum(products[:, m * DH : (m + 1) * DH], axis=1, keepdims=True) * DH ** (-0.5)
        for m in range(2 * heads)
    ]

    for k in range(1, seq_count):
        query_copy(me, lax.rem(me + seq_count - k, seq_count), k - 1).wait_recv()

    gathered = all_query[...].reshape(seq_count * ROWS, half)
    column = lax.broadcasted_iota(jnp.int32, (ROWS, seq_count * ROWS), 1)
    owner_wide = owner[:, :1]
    picks = []
    for part in range(2):
        local = (column & (ROWS - 1)) - part * req_count
        request = (column >> 4) * req_count + local
        hit = (local >= 0) & (local < req_count) & (request == owner_wide)
        pick = jnp.where(hit, 1.0, 0.0).astype(jnp.bfloat16)
        picks.append(jnp.dot(pick, gathered, preferred_element_type=jnp.float32))
    slot_query = jnp.concatenate(picks, axis=1)

    code = owner + 1
    id_high = (code >> 4).astype(jnp.float32)
    id_low = (code & 15).astype(jnp.float32)

    def term_copy(block, target, source):
        return pltpu.make_async_remote_copy(
            src_ref=term_out.at[block],
            dst_ref=term_in.at[source],
            send_sem=term_send.at[target],
            recv_sem=term_recv.at[source],
            device_id={"seq": target},
            device_id_type=MESH,
        )

    contract_last = (((1,), (1,)), ((), ()))
    for h in range(heads):
        maps = slot_query[:, h * 2 * DH : (h + 1) * 2 * DH]
        blank = jnp.zeros((ROWS, DH), jnp.float32)
        spread = jnp.concatenate(
            [
                jnp.concatenate([maps[:, :DH], blank], axis=1),
                jnp.concatenate([blank, maps[:, DH:]], axis=1),
            ],
            axis=0,
        ).astype(jnp.bfloat16)
        loads[h][0].wait()
        loads[h][1].wait()
        pool_scores = lax.dot_general(
            spread,
            key_buf[h].reshape(pool_cells, 2 * DH),
            contract_last,
            preferred_element_type=jnp.float32,
        )
        long_scores = lax.dot_general(
            spread,
            long_key_buf[h].reshape(long_count * long_cells, 2 * DH),
            contract_last,
            preferred_element_type=jnp.float32,
        )
        bias = bias_buf[...]
        bias = jnp.concatenate([bias, bias], axis=0)
        pool_scores = pool_scores * DH ** (-0.5) + bias[:, :pool_cells]
        long_scores = long_scores * DH ** (-0.5) + bias[:, pool_cells:]
        best = jnp.maximum(
            jnp.max(pool_scores, axis=1, keepdims=True),
            jnp.max(long_scores, axis=1, keepdims=True),
        )
        pool_w = jnp.exp(pool_scores - best)
        long_w = jnp.exp(long_scores - best)
        total = jnp.sum(pool_w, axis=1, keepdims=True) + jnp.sum(long_w, axis=1, keepdims=True)
        loads[h][2].wait()
        loads[h][3].wait()
        numer = jnp.dot(
            pool_w.astype(jnp.bfloat16),
            value_buf[h].reshape(pool_cells, DV),
            preferred_element_type=jnp.float32,
        ) + jnp.dot(
            long_w.astype(jnp.bfloat16),
            long_value_buf[h].reshape(long_count * long_cells, DV),
            preferred_element_type=jnp.float32,
        )
        some = best > 0.5 * MASKED
        mean = jnp.where(some, numer / total, 0.0)
        level = jnp.where(some, best + jnp.log(total), MASKED)
        for j in range(2):
            rows = slice(j * ROWS, (j + 1) * ROWS)
            meta = lane_pack(lane, (*split3(level[rows]), id_high, id_low))
            for c in range(2):
                block = (h * 2 + j) * 2 + c
                term_out[block] = jnp.concatenate(
                    [mean[rows, c * LANES : (c + 1) * LANES], meta], axis=0
                ).astype(jnp.bfloat16)
                for g in range(groups):
                    target = g * blocks + block

                    @pl.when(me != target)
                    def _():
                        term_copy(block, target, me).start()

                    @pl.when(me == target)
                    def _():
                        term_in[target] = term_out[block]

    for k in range(1, seq_count):
        source = lax.rem(me + seq_count - k, seq_count)
        term_copy(0, me, source).wait_recv()

    terms = term_in[...]
    means = terms[:, :ROWS].reshape(seq_count * ROWS, LANES)
    meta = jnp.transpose(terms[:, ROWS:].reshape(seq_count * ROWS, LANES).astype(jnp.float32))
    level = (meta[2:3] + meta[1:2]) + meta[0:1]
    ids = (meta[3:4] * 16.0 + meta[4:5]).astype(jnp.int32) - 1
    handled = blocks * req_count
    request = group * handled + lax.broadcasted_iota(
        jnp.int32, (handled, seq_count * ROWS), 0
    )
    member = request == ids
    top = jnp.max(jnp.where(member, level, MASKED), axis=1, keepdims=True)
    factor = jnp.where(member, jnp.exp(jnp.where(member, level - top, 0.0)), 0.0)
    total = jnp.sum(factor, axis=1, keepdims=True)
    high = factor.astype(jnp.bfloat16)
    low = (factor - high.astype(jnp.float32)).astype(jnp.bfloat16)
    merged = jnp.dot(high, means, preferred_element_type=jnp.float32) + jnp.dot(
        low, means, preferred_element_type=jnp.float32
    )
    some = total > 0.0
    safe = jnp.where(some, total, 1.0)
    merged = merged / safe
    level = jnp.where(some, top + jnp.log(safe), MASKED)
    wide = lax.broadcasted_iota(jnp.int32, (handled, LANES), 1)
    meta = lane_pack(wide, split3(level))
    attn_out[...] = jnp.concatenate(
        [
            merged.reshape(blocks, req_count, LANES),
            meta.reshape(blocks, req_count, LANES),
        ],
        axis=1,
    ).astype(jnp.bfloat16)

    def attn_copy(home, source_block):
        return pltpu.make_async_remote_copy(
            src_ref=attn_out.at[home],
            dst_ref=attn_in.at[source_block],
            send_sem=attn_send.at[home],
            recv_sem=attn_recv.at[source_block],
            device_id={"seq": group * blocks + home},
            device_id_type=MESH,
        )

    for k in range(1, blocks):
        attn_copy(lax.rem(block_me + k, blocks), block_me).start()
    attn_in[block_me] = attn_out[block_me]
    weight_load.wait()
    for k in range(1, blocks):
        attn_copy(block_me, lax.rem(block_me + blocks - k, blocks)).wait_recv()

    value = new_value_ref[...].astype(jnp.float32)
    normed = []
    for h in range(heads):
        diffs = []
        for c in range(2):
            attn = []
            for j in range(2):
                got = attn_in[(h * 2 + j) * 2 + c].astype(jnp.float32)
                info = got[req_count:]
                level = (info[:, 2:3] + info[:, 1:2]) + info[:, 0:1]
                score = own_scores[2 * h + j]
                top = jnp.maximum(score, level)
                own_w = jnp.exp(score - top)
                kept_w = jnp.exp(level - top)
                at = h * DV + c * LANES
                attn.append(
                    (own_w * value[:, at : at + LANES] + kept_w * got[:req_count])
                    / (own_w + kept_w)
                )
            diffs.append(attn[0] - lambda_ref[h] * attn[1])
        diff = jnp.concatenate(diffs, axis=1)
        square = jnp.sum(diff * diff, axis=1, keepdims=True) * (1.0 / DV)
        normed.append(
            diff * lax.rsqrt(square + 1e-05) * gain_ref[:, h * DV : (h + 1) * DV]
        )
    normed = jnp.concatenate(normed, axis=1).astype(jnp.bfloat16)

    def part_copy(target, source):
        return pltpu.make_async_remote_copy(
            src_ref=part_out.at[target],
            dst_ref=part_in.at[source],
            send_sem=part_send.at[target],
            recv_sem=part_recv.at[source],
            device_id={"tp": target},
            device_id_type=MESH,
        )

    def partial_out(target):
        cols = pl.ds(pl.multiple_of(target * out_cols, LANES), out_cols)
        return jnp.dot(normed, weight_buf[:, cols], preferred_element_type=jnp.float32)

    for k in range(1, tp_count):
        target = lax.rem(tp_me + k, tp_count)
        part_out[target] = partial_out(target)
        part_copy(target, tp_me).start()
    result = partial_out(tp_me)
    for k in range(1, tp_count):
        source = lax.rem(tp_me + tp_count - k, tp_count)
        part_copy(tp_me, source).wait_recv()
        result = result + part_in[source]
    out_ref[...] = result.astype(jnp.bfloat16)

    for k in range(1, seq_count):
        query_copy(lax.rem(me + k, seq_count), me, k - 1).wait_send()
        term_copy(0, lax.rem(me + k, seq_count), me).wait_send()
    for k in range(1, blocks):
        attn_copy(lax.rem(block_me + k, blocks), block_me).wait_send()
    for k in range(1, tp_count):
        part_copy(lax.rem(tp_me + k, tp_count), tp_me).wait_send()


def on_device(
    seq_count,
    tp_count,
    query,
    new_key,
    new_value,
    key_pool,
    value_pool,
    long_key,
    long_value,
    serve_table,
    serve_len,
    page_slot,
    page_offset,
    long_request,
    long_len,
    lambda_head,
    norm_gain,
    out_weight,
):
    heads = lambda_head.shape[0]
    req_count = query.shape[0]
    blocks = heads * 2 * DV // LANES
    pages = key_pool.shape[0]
    long_count, long_cells = long_key.shape[:2]
    out_cols = out_weight.shape[1] // tp_count
    cells = pages * PG + long_count * long_cells
    smem = pl.BlockSpec(memory_space=pltpu.SMEM)
    vmem = pl.BlockSpec(memory_space=pltpu.VMEM)
    hbm = pl.BlockSpec(memory_space=pl.ANY)
    bf16, f32 = jnp.bfloat16, jnp.float32
    dma = pltpu.SemaphoreType.DMA
    return pl.pallas_call(
        functools.partial(kernel, seq_count, tp_count, heads),
        out_shape=jax.ShapeDtypeStruct((req_count, out_cols), bf16),
        in_specs=[smem] * 7 + [vmem] * 4 + [hbm] * 5,
        out_specs=vmem,
        scratch_shapes=[
            pltpu.VMEM((heads, pages, PG, 2 * DH), bf16),
            pltpu.VMEM((heads, pages, PG, DV), bf16),
            pltpu.VMEM((heads, long_count, long_cells, 2 * DH), bf16),
            pltpu.VMEM((heads, long_count, long_cells, DV), bf16),
            pltpu.VMEM(out_weight.shape, bf16),
            pltpu.VMEM((ROWS, cells), f32),
            pltpu.VMEM((2 * req_count, query.shape[1] // 2), bf16),
            pltpu.VMEM((seq_count, 2 * req_count, query.shape[1] // 2), bf16),
            pltpu.VMEM((blocks, 2 * ROWS, LANES), bf16),
            pltpu.VMEM((seq_count, 2 * ROWS, LANES), bf16),
            pltpu.VMEM((blocks, 2 * req_count, LANES), bf16),
            pltpu.VMEM((blocks, 2 * req_count, LANES), bf16),
            pltpu.VMEM((tp_count, req_count, out_cols), f32),
            pltpu.VMEM((tp_count, req_count, out_cols), f32),
            dma((4 * heads + 1,)),
            dma((seq_count,)),
            dma((seq_count,)),
            dma((seq_count,)),
            dma((seq_count,)),
            dma((blocks,)),
            dma((blocks,)),
            dma((tp_count,)),
            dma((tp_count,)),
        ],
        compiler_params=pltpu.CompilerParams(
            collective_id=0, has_side_effects=True, vmem_limit_bytes=48 * 1024 * 1024
        ),
        cost_estimate=pl.CostEstimate(
            flops=4 * 32 * cells * heads * DV + 2 * req_count * out_weight.size,
            bytes_accessed=4 * (key_pool.size + long_key.size) + 2 * out_weight.size,
            transcendentals=32 * cells * heads,
        ),
        name="decode",
    )(
        serve_table,
        serve_len,
        page_slot,
        page_offset,
        long_request,
        long_len,
        lambda_head,
        query,
        new_key,
        new_value,
        norm_gain.reshape(1, -1),
        key_pool,
        value_pool,
        long_key,
        long_value,
        out_weight,
    )


def solution(mesh):
    return jax.shard_map(
        functools.partial(on_device, mesh.shape["seq"], mesh.shape["tp"]),
        mesh=mesh,
        in_specs=(
            P("seq", "tp"),
            P("seq", "tp"),
            P("seq", "tp"),
            P("seq", None, "tp"),
            P("seq", None, "tp"),
            P(None, "seq", "tp"),
            P(None, "seq", "tp"),
            P("seq"),
            P("seq"),
            P("seq"),
            P("seq"),
            P(),
            P(),
            P("tp"),
            P("tp"),
            P("tp", None),
        ),
        out_specs=P("seq", "tp"),
        check_vma=False,
    )
```

```python
import functools

import jax
import jax.numpy as jnp
from jax import lax
from jax.experimental import pallas as pl
from jax.experimental.pallas import tpu as pltpu
from jax.sharding import PartitionSpec as P

DH = 128
DV = 256
PG = 64
LANES = 128
ROWS = 16
MASKED = -1e30
MESH = pl.DeviceIdType.MESH


def split3(x):
    high = x.astype(jnp.bfloat16).astype(jnp.float32)
    rest = x - high
    mid = rest.astype(jnp.bfloat16).astype(jnp.float32)
    return high, mid, rest - mid


def lane_pack(lane, columns):
    packed = jnp.zeros(lane.shape, jnp.float32)
    for at, column in enumerate(columns):
        packed = jnp.where(lane == at, column, packed)
    return packed


def kernel(
    seq_count,
    tp_count,
    heads,
    table_hbm,
    len_hbm,
    slot_hbm,
    offset_hbm,
    long_request_hbm,
    long_len_hbm,
    lambda_hbm,
    query_hbm,
    new_key_hbm,
    new_value_hbm,
    gain_hbm,
    key_ref,
    value_ref,
    long_key_ref,
    long_value_ref,
    weight_ref,
    out_ref,
    table_ref,
    len_ref,
    slot_ref,
    offset_ref,
    long_request_ref,
    long_len_ref,
    lambda_ref,
    query_ref,
    new_key_ref,
    new_value_ref,
    gain_ref,
    key_buf,
    value_buf,
    long_key_buf,
    long_value_buf,
    weight_buf,
    bias_buf,
    own_query,
    all_query,
    term_out,
    term_in,
    attn_out,
    attn_in,
    part_out,
    part_in,
    load_sem,
    query_send,
    query_recv,
    term_send,
    term_recv,
    attn_send,
    attn_recv,
    part_send,
    part_recv,
    small_sem,
):
    me = lax.axis_index("seq")
    tp_me = lax.axis_index("tp")
    blocks = heads * 2 * DV // LANES
    group = me // blocks
    block_me = me % blocks
    req_count = query_ref.shape[0]
    serve_count = table_ref.shape[0]
    page_count = slot_ref.shape[0]
    long_count = long_request_ref.shape[0]
    long_cells = long_key_ref.shape[1]
    pool_cells = page_count * PG
    out_cols = weight_ref.shape[1] // tp_count

    loads = []
    for h in range(heads):
        cols = pl.ds(h * 2 * DH, 2 * DH)
        row = []
        for at, (src, dst) in enumerate(
            (
                (key_ref, key_buf),
                (long_key_ref, long_key_buf),
                (value_ref, value_buf),
                (long_value_ref, long_value_buf),
            )
        ):
            row.append(
                pltpu.make_async_copy(src.at[:, :, cols], dst.at[h], load_sem.at[4 * h + at])
            )
        loads.append(row)
    weight_load = pltpu.make_async_copy(weight_ref, weight_buf, load_sem.at[4 * heads])

    smalls = [
        pltpu.make_async_copy(src, dst, small_sem.at[at])
        for at, (src, dst) in enumerate(
            (
                (query_hbm, query_ref),
                (table_hbm, table_ref),
                (len_hbm, len_ref),
                (slot_hbm, slot_ref),
                (offset_hbm, offset_ref),
                (long_request_hbm, long_request_ref),
                (long_len_hbm, long_len_ref),
                (new_key_hbm, new_key_ref),
                (lambda_hbm, lambda_ref),
                (new_value_hbm, new_value_ref),
                (gain_hbm, gain_ref),
            )
        )
    ]
    smalls[0].start()
    barrier = pltpu.get_barrier_semaphore()
    for k in range(1, seq_count):
        pl.semaphore_signal(
            barrier, inc=1, device_id={"seq": lax.rem(me + k, seq_count)}, device_id_type=MESH
        )
    for k in range(1, tp_count):
        pl.semaphore_signal(
            barrier, inc=1, device_id={"tp": lax.rem(tp_me + k, tp_count)}, device_id_type=MESH
        )
    for copy in smalls[1:]:
        copy.start()
    for row in loads:
        row[0].start()
        row[1].start()
    smalls[0].wait()

    query = query_ref[...].astype(jnp.float32)
    half = query.shape[1] // 2
    own_query[...] = jnp.concatenate([query[:, :half], query[:, half:]], axis=0).astype(
        jnp.bfloat16
    )
    all_query[me] = own_query[...]
    pl.semaphore_wait(barrier, seq_count + tp_count - 2)

    def query_copy(target, owner, at):
        return pltpu.make_async_remote_copy(
            src_ref=own_query,
            dst_ref=all_query.at[owner],
            send_sem=query_send.at[at],
            recv_sem=query_recv.at[owner],
            device_id={"seq": target},
            device_id_type=MESH,
        )

    for k in range(1, seq_count):
        query_copy(lax.rem(me + k, seq_count), me, k - 1).start()

    for row in loads:
        row[2].start()
        row[3].start()
    weight_load.start()
    for copy in smalls[1:]:
        copy.wait()

    lane = lax.broadcasted_iota(jnp.int32, (ROWS, LANES), 1)
    slot_row = lax.broadcasted_iota(jnp.int32, (ROWS, LANES), 0)
    length = jnp.zeros((ROWS, LANES), jnp.int32)
    owner = jnp.full((ROWS, LANES), -1, jnp.int32)
    for s in range(serve_count):
        length = jnp.where(slot_row == s, len_ref[s], length)
        owner = jnp.where(slot_row == s, table_ref[s], owner)
    for n in range(long_count):
        owner = jnp.where(slot_row == serve_count + n, long_request_ref[n], owner)
    per_chunk = LANES // PG
    for chunk in range(pool_cells // LANES):
        slot = jnp.full((ROWS, LANES), slot_ref[chunk * per_chunk], jnp.int32)
        offset = jnp.full((ROWS, LANES), offset_ref[chunk * per_chunk], jnp.int32)
        for extra in range(1, per_chunk):
            beyond = lane >= extra * PG
            slot = jnp.where(beyond, slot_ref[chunk * per_chunk + extra], slot)
            offset = jnp.where(beyond, offset_ref[chunk * per_chunk + extra], offset)
        live = (slot == slot_row) & (offset + (lane & (PG - 1)) < length)
        bias_buf[:, chunk * LANES : (chunk + 1) * LANES] = jnp.where(live, 0.0, MASKED)
    for n in range(long_count):
        for chunk in range(long_cells // LANES):
            pos = me * long_cells + chunk * LANES + lane
            live = (slot_row == serve_count + n) & (pos < long_len_ref[n])
            start = pool_cells + n * long_cells + chunk * LANES
            bias_buf[:, start : start + LANES] = jnp.where(live, 0.0, MASKED)

    products = query * new_key_ref[...].astype(jnp.float32)
    own_scores = [
        jnp.sum(products[:, m * DH : (m + 1) * DH], axis=1, keepdims=True) * DH ** (-0.5)
        for m in range(2 * heads)
    ]

    for row in loads:
        for copy in row:
            copy.wait()
    for k in range(1, seq_count):
        query_copy(me, lax.rem(me + seq_count - k, seq_count), k - 1).wait_recv()

    gathered = all_query[...].reshape(seq_count * ROWS, half)
    column = lax.broadcasted_iota(jnp.int32, (ROWS, seq_count * ROWS), 1)
    owner_wide = owner[:, :1]
    picks = []
    for part in range(2):
        local = (column & (ROWS - 1)) - part * req_count
        request = (column >> 4) * req_count + local
        hit = (local >= 0) & (local < req_count) & (request == owner_wide)
        pick = jnp.where(hit, 1.0, 0.0).astype(jnp.bfloat16)
        picks.append(jnp.dot(pick, gathered, preferred_element_type=jnp.float32))
    slot_query = jnp.concatenate(picks, axis=1)

    code = owner + 1
    id_high = (code >> 4).astype(jnp.float32)
    id_low = (code & 15).astype(jnp.float32)

    def term_copy(block, target, source):
        return pltpu.make_async_remote_copy(
            src_ref=term_out.at[block],
            dst_ref=term_in.at[source],
            send_sem=term_send.at[target],
            recv_sem=term_recv.at[source],
            device_id={"seq": target},
            device_id_type=MESH,
        )

    contract_last = (((1,), (1,)), ((), ()))
    for h in range(heads):
        maps = slot_query[:, h * 2 * DH : (h + 1) * 2 * DH]
        blank = jnp.zeros((ROWS, DH), jnp.float32)
        spread = jnp.concatenate(
            [
                jnp.concatenate([maps[:, :DH], blank], axis=1),
                jnp.concatenate([blank, maps[:, DH:]], axis=1),
            ],
            axis=0,
        ).astype(jnp.bfloat16)
        pool_scores = lax.dot_general(
            spread,
            key_buf[h].reshape(pool_cells, 2 * DH),
            contract_last,
            preferred_element_type=jnp.float32,
        )
        long_scores = lax.dot_general(
            spread,
            long_key_buf[h].reshape(long_count * long_cells, 2 * DH),
            contract_last,
            preferred_element_type=jnp.float32,
        )
        bias = bias_buf[...]
        bias = jnp.concatenate([bias, bias], axis=0)
        pool_scores = pool_scores * DH ** (-0.5) + bias[:, :pool_cells]
        long_scores = long_scores * DH ** (-0.5) + bias[:, pool_cells:]
        best = jnp.maximum(
            jnp.max(pool_scores, axis=1, keepdims=True),
            jnp.max(long_scores, axis=1, keepdims=True),
        )
        pool_w = jnp.exp(pool_scores - best)
        long_w = jnp.exp(long_scores - best)
        total = jnp.sum(pool_w, axis=1, keepdims=True) + jnp.sum(long_w, axis=1, keepdims=True)
        numer = jnp.dot(
            pool_w.astype(jnp.bfloat16),
            value_buf[h].reshape(pool_cells, DV),
            preferred_element_type=jnp.float32,
        ) + jnp.dot(
            long_w.astype(jnp.bfloat16),
            long_value_buf[h].reshape(long_count * long_cells, DV),
            preferred_element_type=jnp.float32,
        )
        some = best > 0.5 * MASKED
        mean = jnp.where(some, numer / total, 0.0)
        level = jnp.where(some, best + jnp.log(total), MASKED)
        for j in range(2):
            rows = slice(j * ROWS, (j + 1) * ROWS)
            meta = lane_pack(lane, (*split3(level[rows]), id_high, id_low))
            for c in range(2):
                block = (h * 2 + j) * 2 + c
                term_out[block] = jnp.concatenate(
                    [mean[rows, c * LANES : (c + 1) * LANES], meta], axis=0
                ).astype(jnp.bfloat16)

    for k in range(1, seq_count):
        target = lax.rem(me + k, seq_count)
        term_copy(lax.rem(target, blocks), target, me).start()
    term_in[me] = term_out[block_me]
    for k in range(1, seq_count):
        source = lax.rem(me + seq_count - k, seq_count)
        term_copy(0, me, source).wait_recv()

    terms = term_in[...]
    means = terms[:, :ROWS].reshape(seq_count * ROWS, LANES)
    meta = jnp.transpose(terms[:, ROWS:].reshape(seq_count * ROWS, LANES).astype(jnp.float32))
    level = (meta[2:3] + meta[1:2]) + meta[0:1]
    ids = (meta[3:4] * 16.0 + meta[4:5]).astype(jnp.int32) - 1
    handled = blocks * req_count
    request = group * handled + lax.broadcasted_iota(
        jnp.int32, (handled, seq_count * ROWS), 0
    )
    member = request == ids
    top = jnp.max(jnp.where(member, level, MASKED), axis=1, keepdims=True)
    factor = jnp.where(member, jnp.exp(jnp.where(member, level - top, 0.0)), 0.0)
    total = jnp.sum(factor, axis=1, keepdims=True)
    high = factor.astype(jnp.bfloat16)
    low = (factor - high.astype(jnp.float32)).astype(jnp.bfloat16)
    merged = jnp.dot(high, means, preferred_element_type=jnp.float32) + jnp.dot(
        low, means, preferred_element_type=jnp.float32
    )
    some = total > 0.0
    safe = jnp.where(some, total, 1.0)
    merged = merged / safe
    level = jnp.where(some, top + jnp.log(safe), MASKED)
    wide = lax.broadcasted_iota(jnp.int32, (handled, LANES), 1)
    meta = lane_pack(wide, split3(level))
    attn_out[...] = jnp.concatenate(
        [
            merged.reshape(blocks, req_count, LANES),
            meta.reshape(blocks, req_count, LANES),
        ],
        axis=1,
    ).astype(jnp.bfloat16)

    def attn_copy(home, source_block):
        return pltpu.make_async_remote_copy(
            src_ref=attn_out.at[home],
            dst_ref=attn_in.at[source_block],
            send_sem=attn_send.at[home],
            recv_sem=attn_recv.at[source_block],
            device_id={"seq": group * blocks + home},
            device_id_type=MESH,
        )

    for k in range(1, blocks):
        attn_copy(lax.rem(block_me + k, blocks), block_me).start()
    attn_in[block_me] = attn_out[block_me]
    weight_load.wait()
    for k in range(1, blocks):
        attn_copy(block_me, lax.rem(block_me + blocks - k, blocks)).wait_recv()

    value = new_value_ref[...].astype(jnp.float32)
    normed = []
    for h in range(heads):
        diffs = []
        for c in range(2):
            attn = []
            for j in range(2):
                got = attn_in[(h * 2 + j) * 2 + c].astype(jnp.float32)
                info = got[req_count:]
                level = (info[:, 2:3] + info[:, 1:2]) + info[:, 0:1]
                score = own_scores[2 * h + j]
                top = jnp.maximum(score, level)
                own_w = jnp.exp(score - top)
                kept_w = jnp.exp(level - top)
                at = h * DV + c * LANES
                attn.append(
                    (own_w * value[:, at : at + LANES] + kept_w * got[:req_count])
                    / (own_w + kept_w)
                )
            diffs.append(attn[0] - lambda_ref[h] * attn[1])
        diff = jnp.concatenate(diffs, axis=1)
        square = jnp.sum(diff * diff, axis=1, keepdims=True) * (1.0 / DV)
        normed.append(
            diff * lax.rsqrt(square + 1e-05) * gain_ref[:, h * DV : (h + 1) * DV]
        )
    normed = jnp.concatenate(normed, axis=1).astype(jnp.bfloat16)

    def part_copy(target, source):
        return pltpu.make_async_remote_copy(
            src_ref=part_out.at[target],
            dst_ref=part_in.at[source],
            send_sem=part_send.at[target],
            recv_sem=part_recv.at[source],
            device_id={"tp": target},
            device_id_type=MESH,
        )

    def partial_out(target):
        cols = pl.ds(pl.multiple_of(target * out_cols, LANES), out_cols)
        return jnp.dot(normed, weight_buf[:, cols], preferred_element_type=jnp.float32)

    for k in range(1, tp_count):
        target = lax.rem(tp_me + k, tp_count)
        part_out[target] = partial_out(target)
        part_copy(target, tp_me).start()
    result = partial_out(tp_me)
    for k in range(1, tp_count):
        source = lax.rem(tp_me + tp_count - k, tp_count)
        part_copy(tp_me, source).wait_recv()
        result = result + part_in[source]
    out_ref[...] = result.astype(jnp.bfloat16)

    for k in range(1, seq_count):
        query_copy(lax.rem(me + k, seq_count), me, k - 1).wait_send()
        term_copy(0, lax.rem(me + k, seq_count), me).wait_send()
    for k in range(1, blocks):
        attn_copy(lax.rem(block_me + k, blocks), block_me).wait_send()
    for k in range(1, tp_count):
        part_copy(lax.rem(tp_me + k, tp_count), tp_me).wait_send()


def on_device(
    seq_count,
    tp_count,
    query,
    new_key,
    new_value,
    key_pool,
    value_pool,
    long_key,
    long_value,
    serve_table,
    serve_len,
    page_slot,
    page_offset,
    long_request,
    long_len,
    lambda_head,
    norm_gain,
    out_weight,
):
    heads = lambda_head.shape[0]
    req_count = query.shape[0]
    blocks = heads * 2 * DV // LANES
    pages = key_pool.shape[0]
    long_count, long_cells = long_key.shape[:2]
    out_cols = out_weight.shape[1] // tp_count
    cells = pages * PG + long_count * long_cells
    vmem = pl.BlockSpec(memory_space=pltpu.VMEM)
    hbm = pl.BlockSpec(memory_space=pl.ANY)
    bf16, f32 = jnp.bfloat16, jnp.float32
    dma = pltpu.SemaphoreType.DMA
    return pl.pallas_call(
        functools.partial(kernel, seq_count, tp_count, heads),
        out_shape=jax.ShapeDtypeStruct((req_count, out_cols), bf16),
        in_specs=[hbm] * 16,
        out_specs=vmem,
        scratch_shapes=[
            pltpu.SMEM(serve_table.shape, jnp.int32),
            pltpu.SMEM(serve_len.shape, jnp.int32),
            pltpu.SMEM(page_slot.shape, jnp.int32),
            pltpu.SMEM(page_offset.shape, jnp.int32),
            pltpu.SMEM(long_request.shape, jnp.int32),
            pltpu.SMEM(long_len.shape, jnp.int32),
            pltpu.SMEM(lambda_head.shape, f32),
            pltpu.VMEM(query.shape, bf16),
            pltpu.VMEM(new_key.shape, bf16),
            pltpu.VMEM(new_value.shape, bf16),
            pltpu.VMEM((1, norm_gain.size), f32),
            pltpu.VMEM((heads, pages, PG, 2 * DH), bf16),
            pltpu.VMEM((heads, pages, PG, DV), bf16),
            pltpu.VMEM((heads, long_count, long_cells, 2 * DH), bf16),
            pltpu.VMEM((heads, long_count, long_cells, DV), bf16),
            pltpu.VMEM(out_weight.shape, bf16),
            pltpu.VMEM((ROWS, cells), f32),
            pltpu.VMEM((2 * req_count, query.shape[1] // 2), bf16),
            pltpu.VMEM((seq_count, 2 * req_count, query.shape[1] // 2), bf16),
            pltpu.VMEM((blocks, 2 * ROWS, LANES), bf16),
            pltpu.VMEM((seq_count, 2 * ROWS, LANES), bf16),
            pltpu.VMEM((blocks, 2 * req_count, LANES), bf16),
            pltpu.VMEM((blocks, 2 * req_count, LANES), bf16),
            pltpu.VMEM((tp_count, req_count, out_cols), f32),
            pltpu.VMEM((tp_count, req_count, out_cols), f32),
            dma((4 * heads + 1,)),
            dma((seq_count,)),
            dma((seq_count,)),
            dma((seq_count,)),
            dma((seq_count,)),
            dma((blocks,)),
            dma((blocks,)),
            dma((tp_count,)),
            dma((tp_count,)),
            dma((11,)),
        ],
        compiler_params=pltpu.CompilerParams(
            collective_id=0, has_side_effects=True, vmem_limit_bytes=64 * 1024 * 1024
        ),
        cost_estimate=pl.CostEstimate(
            flops=4 * 32 * cells * heads * DV + 2 * req_count * out_weight.size,
            bytes_accessed=4 * (key_pool.size + long_key.size) + 2 * out_weight.size,
            transcendentals=32 * cells * heads,
        ),
        name="decode",
    )(
        serve_table,
        serve_len,
        page_slot,
        page_offset,
        long_request,
        long_len,
        lambda_head,
        query,
        new_key,
        new_value,
        norm_gain.reshape(1, -1),
        key_pool,
        value_pool,
        long_key,
        long_value,
        out_weight,
    )


def solution(mesh):
    return jax.shard_map(
        functools.partial(on_device, mesh.shape["seq"], mesh.shape["tp"]),
        mesh=mesh,
        in_specs=(
            P("seq", "tp"),
            P("seq", "tp"),
            P("seq", "tp"),
            P("seq", None, "tp"),
            P("seq", None, "tp"),
            P(None, "seq", "tp"),
            P(None, "seq", "tp"),
            P("seq"),
            P("seq"),
            P("seq"),
            P("seq"),
            P(),
            P(),
            P("tp"),
            P("tp"),
            P("tp", None),
        ),
        out_specs=P("seq", "tp"),
        check_vma=False,
    )
```

```python
import functools

import jax
import jax.numpy as jnp
from jax import lax
from jax.experimental import pallas as pl
from jax.experimental.pallas import tpu as pltpu
from jax.sharding import PartitionSpec as P

DH = 128
DV = 256
PG = 64
LANES = 128
ROWS = 16
MASKED = -1e30
MESH = pl.DeviceIdType.MESH


def split3(x):
    high = x.astype(jnp.bfloat16).astype(jnp.float32)
    rest = x - high
    mid = rest.astype(jnp.bfloat16).astype(jnp.float32)
    return high, mid, rest - mid


def lane_pack(lane, columns):
    packed = jnp.zeros(lane.shape, jnp.float32)
    for at, column in enumerate(columns):
        packed = jnp.where(lane == at, column, packed)
    return packed


def kernel(
    seq_count,
    tp_count,
    heads,
    table_hbm,
    len_hbm,
    slot_hbm,
    offset_hbm,
    long_request_hbm,
    long_len_hbm,
    lambda_hbm,
    query_hbm,
    new_key_hbm,
    new_value_hbm,
    gain_hbm,
    key_ref,
    value_ref,
    long_key_ref,
    long_value_ref,
    weight_ref,
    out_ref,
    table_ref,
    len_ref,
    slot_ref,
    offset_ref,
    long_request_ref,
    long_len_ref,
    lambda_ref,
    query_ref,
    new_key_ref,
    new_value_ref,
    gain_ref,
    key_buf,
    value_buf,
    long_key_buf,
    long_value_buf,
    weight_buf,
    bias_buf,
    own_query,
    all_query,
    term_out,
    term_in,
    attn_out,
    attn_in,
    part_out,
    part_in,
    load_sem,
    query_send,
    query_recv,
    term_send,
    term_recv,
    attn_send,
    attn_recv,
    part_send,
    part_recv,
    small_sem,
):
    me = lax.axis_index("seq")
    tp_me = lax.axis_index("tp")
    blocks = heads * 2 * DV // LANES
    group = me // blocks
    block_me = me % blocks
    req_count = query_ref.shape[0]
    serve_count = table_ref.shape[0]
    page_count = slot_ref.shape[0]
    long_count = long_request_ref.shape[0]
    long_cells = long_key_ref.shape[1]
    pool_cells = page_count * PG
    out_cols = weight_ref.shape[1] // tp_count
    chunks = own_query.shape[0]
    chunk_heads = heads // chunks
    chunk_blocks = blocks // chunks
    width = chunk_heads * DV

    loads = []
    for h in range(chunks):
        cols = pl.ds(h * width, width)
        row = []
        for at, (src, dst) in enumerate(
            (
                (key_ref, key_buf),
                (long_key_ref, long_key_buf),
                (value_ref, value_buf),
                (long_value_ref, long_value_buf),
            )
        ):
            row.append(
                pltpu.make_async_copy(src.at[:, :, cols], dst.at[h], load_sem.at[4 * h + at])
            )
        loads.append(row)
    weight_load = pltpu.make_async_copy(weight_ref, weight_buf, load_sem.at[4 * chunks])

    smalls = [
        pltpu.make_async_copy(src, dst, small_sem.at[at])
        for at, (src, dst) in enumerate(
            (
                (query_hbm, query_ref),
                (table_hbm, table_ref),
                (len_hbm, len_ref),
                (slot_hbm, slot_ref),
                (offset_hbm, offset_ref),
                (long_request_hbm, long_request_ref),
                (long_len_hbm, long_len_ref),
                (new_key_hbm, new_key_ref),
                (lambda_hbm, lambda_ref),
                (new_value_hbm, new_value_ref),
                (gain_hbm, gain_ref),
            )
        )
    ]
    smalls[0].start()
    barrier = pltpu.get_barrier_semaphore()
    for k in range(1, seq_count):
        pl.semaphore_signal(
            barrier, inc=1, device_id={"seq": lax.rem(me + k, seq_count)}, device_id_type=MESH
        )
    for k in range(1, tp_count):
        pl.semaphore_signal(
            barrier, inc=1, device_id={"tp": lax.rem(tp_me + k, tp_count)}, device_id_type=MESH
        )
    for copy in smalls[1:]:
        copy.start()
    for copy in loads[0]:
        copy.start()
    smalls[0].wait()

    query = query_ref[...].astype(jnp.float32)
    half = width // 2
    for p in range(chunks):
        at = p * width
        packed = jnp.concatenate(
            [query[:, at : at + half], query[:, at + half : at + width]], axis=0
        ).astype(jnp.bfloat16)
        own_query[p] = packed
        all_query[p, me] = packed
    pl.semaphore_wait(barrier, seq_count + tp_count - 2)

    def query_copy(p, target, owner, at):
        return pltpu.make_async_remote_copy(
            src_ref=own_query.at[p],
            dst_ref=all_query.at[p, owner],
            send_sem=query_send.at[p, at],
            recv_sem=query_recv.at[p, owner],
            device_id={"seq": target},
            device_id_type=MESH,
        )

    for p in range(chunks):
        for k in range(1, seq_count):
            query_copy(p, lax.rem(me + k, seq_count), me, k - 1).start()

    for row in loads[1:]:
        for copy in row:
            copy.start()
    weight_load.start()
    for copy in smalls[1:]:
        copy.wait()

    lane = lax.broadcasted_iota(jnp.int32, (ROWS, LANES), 1)
    slot_row = lax.broadcasted_iota(jnp.int32, (ROWS, LANES), 0)
    length = jnp.zeros((ROWS, LANES), jnp.int32)
    owner = jnp.full((ROWS, LANES), -1, jnp.int32)
    for s in range(serve_count):
        length = jnp.where(slot_row == s, len_ref[s], length)
        owner = jnp.where(slot_row == s, table_ref[s], owner)
    for n in range(long_count):
        owner = jnp.where(slot_row == serve_count + n, long_request_ref[n], owner)
    per_chunk = LANES // PG
    for chunk in range(pool_cells // LANES):
        slot = jnp.full((ROWS, LANES), slot_ref[chunk * per_chunk], jnp.int32)
        offset = jnp.full((ROWS, LANES), offset_ref[chunk * per_chunk], jnp.int32)
        for extra in range(1, per_chunk):
            beyond = lane >= extra * PG
            slot = jnp.where(beyond, slot_ref[chunk * per_chunk + extra], slot)
            offset = jnp.where(beyond, offset_ref[chunk * per_chunk + extra], offset)
        live = (slot == slot_row) & (offset + (lane & (PG - 1)) < length)
        bias_buf[:, chunk * LANES : (chunk + 1) * LANES] = jnp.where(live, 0.0, MASKED)
    for n in range(long_count):
        for chunk in range(long_cells // LANES):
            pos = me * long_cells + chunk * LANES + lane
            live = (slot_row == serve_count + n) & (pos < long_len_ref[n])
            start = pool_cells + n * long_cells + chunk * LANES
            bias_buf[:, start : start + LANES] = jnp.where(live, 0.0, MASKED)

    products = query * new_key_ref[...].astype(jnp.float32)
    own_scores = [
        jnp.sum(products[:, m * DH : (m + 1) * DH], axis=1, keepdims=True) * DH ** (-0.5)
        for m in range(2 * heads)
    ]

    column = lax.broadcasted_iota(jnp.int32, (ROWS, seq_count * ROWS), 1)
    owner_wide = owner[:, :1]
    picks = []
    for part in range(2):
        local = (column & (ROWS - 1)) - part * req_count
        request = (column >> 4) * req_count + local
        hit = (local >= 0) & (local < req_count) & (request == owner_wide)
        picks.append(jnp.where(hit, 1.0, 0.0).astype(jnp.bfloat16))

    code = owner + 1
    id_high = (code >> 4).astype(jnp.float32)
    id_low = (code & 15).astype(jnp.float32)

    def term_copy(block, target, source):
        return pltpu.make_async_remote_copy(
            src_ref=term_out.at[block],
            dst_ref=term_in.at[source],
            send_sem=term_send.at[target],
            recv_sem=term_recv.at[source],
            device_id={"seq": target},
            device_id_type=MESH,
        )

    contract_last = (((1,), (1,)), ((), ()))
    for h in range(heads):
        p, inner = h // chunk_heads, h % chunk_heads
        lanes = slice(inner * DV, (inner + 1) * DV)
        if inner == 0:
            for copy in loads[p]:
                copy.wait()
            for k in range(1, seq_count):
                source = lax.rem(me + seq_count - k, seq_count)
                query_copy(p, me, source, k - 1).wait_recv()
            gathered = all_query[p].reshape(seq_count * ROWS, half)
            slot_query = jnp.concatenate(
                [jnp.dot(pick, gathered, preferred_element_type=jnp.float32) for pick in picks],
                axis=1,
            )
        maps = slot_query[:, lanes]
        blank = jnp.zeros((ROWS, DH), jnp.float32)
        spread = jnp.concatenate(
            [
                jnp.concatenate([maps[:, :DH], blank], axis=1),
                jnp.concatenate([blank, maps[:, DH:]], axis=1),
            ],
            axis=0,
        ).astype(jnp.bfloat16)
        pool_scores = lax.dot_general(
            spread,
            key_buf[p, :, :, lanes].reshape(pool_cells, 2 * DH),
            contract_last,
            preferred_element_type=jnp.float32,
        )
        long_scores = lax.dot_general(
            spread,
            long_key_buf[p, :, :, lanes].reshape(long_count * long_cells, 2 * DH),
            contract_last,
            preferred_element_type=jnp.float32,
        )
        bias = bias_buf[...]
        bias = jnp.concatenate([bias, bias], axis=0)
        pool_scores = pool_scores * DH ** (-0.5) + bias[:, :pool_cells]
        long_scores = long_scores * DH ** (-0.5) + bias[:, pool_cells:]
        best = jnp.maximum(
            jnp.max(pool_scores, axis=1, keepdims=True),
            jnp.max(long_scores, axis=1, keepdims=True),
        )
        pool_w = jnp.exp(pool_scores - best)
        long_w = jnp.exp(long_scores - best)
        total = jnp.sum(pool_w, axis=1, keepdims=True) + jnp.sum(long_w, axis=1, keepdims=True)
        numer = jnp.dot(
            pool_w.astype(jnp.bfloat16),
            value_buf[p, :, :, lanes].reshape(pool_cells, DV),
            preferred_element_type=jnp.float32,
        ) + jnp.dot(
            long_w.astype(jnp.bfloat16),
            long_value_buf[p, :, :, lanes].reshape(long_count * long_cells, DV),
            preferred_element_type=jnp.float32,
        )
        some = best > 0.5 * MASKED
        mean = jnp.where(some, numer / total, 0.0)
        level = jnp.where(some, best + jnp.log(total), MASKED)
        for j in range(2):
            rows = slice(j * ROWS, (j + 1) * ROWS)
            meta = lane_pack(lane, (*split3(level[rows]), id_high, id_low))
            for c in range(2):
                block = (h * 2 + j) * 2 + c
                term_out[block] = jnp.concatenate(
                    [mean[rows, c * LANES : (c + 1) * LANES], meta], axis=0
                ).astype(jnp.bfloat16)
        if inner == chunk_heads - 1:
            for g in range(seq_count // blocks):
                for k in range(chunk_blocks):
                    block = p * chunk_blocks + lax.rem(me + k, chunk_blocks)
                    target = g * blocks + block
                    if k:
                        term_copy(block, target, me).start()
                    else:

                        @pl.when(target != me)
                        def _():
                            term_copy(block, target, me).start()

    term_in[me] = term_out[block_me]
    for k in range(1, seq_count):
        source = lax.rem(me + seq_count - k, seq_count)
        term_copy(0, me, source).wait_recv()

    terms = term_in[...]
    means = terms[:, :ROWS].reshape(seq_count * ROWS, LANES)
    meta = jnp.transpose(terms[:, ROWS:].reshape(seq_count * ROWS, LANES).astype(jnp.float32))
    level = (meta[2:3] + meta[1:2]) + meta[0:1]
    ids = (meta[3:4] * 16.0 + meta[4:5]).astype(jnp.int32) - 1
    handled = blocks * req_count
    request = group * handled + lax.broadcasted_iota(
        jnp.int32, (handled, seq_count * ROWS), 0
    )
    member = request == ids
    top = jnp.max(jnp.where(member, level, MASKED), axis=1, keepdims=True)
    factor = jnp.where(member, jnp.exp(jnp.where(member, level - top, 0.0)), 0.0)
    total = jnp.sum(factor, axis=1, keepdims=True)
    high = factor.astype(jnp.bfloat16)
    low = (factor - high.astype(jnp.float32)).astype(jnp.bfloat16)
    merged = jnp.dot(high, means, preferred_element_type=jnp.float32) + jnp.dot(
        low, means, preferred_element_type=jnp.float32
    )
    some = total > 0.0
    safe = jnp.where(some, total, 1.0)
    merged = merged / safe
    level = jnp.where(some, top + jnp.log(safe), MASKED)
    wide = lax.broadcasted_iota(jnp.int32, (handled, LANES), 1)
    meta = lane_pack(wide, split3(level))
    attn_out[...] = jnp.concatenate(
        [
            merged.reshape(blocks, req_count, LANES),
            meta.reshape(blocks, req_count, LANES),
        ],
        axis=1,
    ).astype(jnp.bfloat16)

    def attn_copy(home, source_block):
        return pltpu.make_async_remote_copy(
            src_ref=attn_out.at[home],
            dst_ref=attn_in.at[source_block],
            send_sem=attn_send.at[home],
            recv_sem=attn_recv.at[source_block],
            device_id={"seq": group * blocks + home},
            device_id_type=MESH,
        )

    for k in range(1, blocks):
        attn_copy(lax.rem(block_me + k, blocks), block_me).start()
    attn_in[block_me] = attn_out[block_me]
    weight_load.wait()
    for k in range(1, blocks):
        attn_copy(block_me, lax.rem(block_me + blocks - k, blocks)).wait_recv()

    value = new_value_ref[...].astype(jnp.float32)
    normed = []
    for h in range(heads):
        diffs = []
        for c in range(2):
            attn = []
            for j in range(2):
                got = attn_in[(h * 2 + j) * 2 + c].astype(jnp.float32)
                info = got[req_count:]
                level = (info[:, 2:3] + info[:, 1:2]) + info[:, 0:1]
                score = own_scores[2 * h + j]
                top = jnp.maximum(score, level)
                own_w = jnp.exp(score - top)
                kept_w = jnp.exp(level - top)
                at = h * DV + c * LANES
                attn.append(
                    (own_w * value[:, at : at + LANES] + kept_w * got[:req_count])
                    / (own_w + kept_w)
                )
            diffs.append(attn[0] - lambda_ref[h] * attn[1])
        diff = jnp.concatenate(diffs, axis=1)
        square = jnp.sum(diff * diff, axis=1, keepdims=True) * (1.0 / DV)
        normed.append(
            diff * lax.rsqrt(square + 1e-05) * gain_ref[:, h * DV : (h + 1) * DV]
        )
    normed = jnp.concatenate(normed, axis=1).astype(jnp.bfloat16)

    def part_copy(target, source):
        return pltpu.make_async_remote_copy(
            src_ref=part_out.at[target],
            dst_ref=part_in.at[source],
            send_sem=part_send.at[target],
            recv_sem=part_recv.at[source],
            device_id={"tp": target},
            device_id_type=MESH,
        )

    def partial_out(target):
        cols = pl.ds(pl.multiple_of(target * out_cols, LANES), out_cols)
        return jnp.dot(normed, weight_buf[:, cols], preferred_element_type=jnp.float32)

    for k in range(1, tp_count):
        target = lax.rem(tp_me + k, tp_count)
        part_out[target] = partial_out(target)
        part_copy(target, tp_me).start()
    result = partial_out(tp_me)
    for k in range(1, tp_count):
        source = lax.rem(tp_me + tp_count - k, tp_count)
        part_copy(tp_me, source).wait_recv()
        result = result + part_in[source]
    out_ref[...] = result.astype(jnp.bfloat16)

    for k in range(1, seq_count):
        for p in range(chunks):
            query_copy(p, lax.rem(me + k, seq_count), me, k - 1).wait_send()
        term_copy(0, lax.rem(me + k, seq_count), me).wait_send()
    for k in range(1, blocks):
        attn_copy(lax.rem(block_me + k, blocks), block_me).wait_send()
    for k in range(1, tp_count):
        part_copy(lax.rem(tp_me + k, tp_count), tp_me).wait_send()


def on_device(
    seq_count,
    tp_count,
    query,
    new_key,
    new_value,
    key_pool,
    value_pool,
    long_key,
    long_value,
    serve_table,
    serve_len,
    page_slot,
    page_offset,
    long_request,
    long_len,
    lambda_head,
    norm_gain,
    out_weight,
):
    heads = lambda_head.shape[0]
    req_count = query.shape[0]
    blocks = heads * 2 * DV // LANES
    pages = key_pool.shape[0]
    long_count, long_cells = long_key.shape[:2]
    out_cols = out_weight.shape[1] // tp_count
    chunks = 2 if heads % 2 == 0 else 1
    width = heads // chunks * DV
    cells = pages * PG + long_count * long_cells
    vmem = pl.BlockSpec(memory_space=pltpu.VMEM)
    hbm = pl.BlockSpec(memory_space=pl.ANY)
    bf16, f32 = jnp.bfloat16, jnp.float32
    dma = pltpu.SemaphoreType.DMA
    return pl.pallas_call(
        functools.partial(kernel, seq_count, tp_count, heads),
        out_shape=jax.ShapeDtypeStruct((req_count, out_cols), bf16),
        in_specs=[hbm] * 16,
        out_specs=vmem,
        scratch_shapes=[
            pltpu.SMEM(serve_table.shape, jnp.int32),
            pltpu.SMEM(serve_len.shape, jnp.int32),
            pltpu.SMEM(page_slot.shape, jnp.int32),
            pltpu.SMEM(page_offset.shape, jnp.int32),
            pltpu.SMEM(long_request.shape, jnp.int32),
            pltpu.SMEM(long_len.shape, jnp.int32),
            pltpu.SMEM(lambda_head.shape, f32),
            pltpu.VMEM(query.shape, bf16),
            pltpu.VMEM(new_key.shape, bf16),
            pltpu.VMEM(new_value.shape, bf16),
            pltpu.VMEM((1, norm_gain.size), f32),
            pltpu.VMEM((chunks, pages, PG, width), bf16),
            pltpu.VMEM((chunks, pages, PG, width), bf16),
            pltpu.VMEM((chunks, long_count, long_cells, width), bf16),
            pltpu.VMEM((chunks, long_count, long_cells, width), bf16),
            pltpu.VMEM(out_weight.shape, bf16),
            pltpu.VMEM((ROWS, cells), f32),
            pltpu.VMEM((chunks, 2 * req_count, width // 2), bf16),
            pltpu.VMEM((chunks, seq_count, 2 * req_count, width // 2), bf16),
            pltpu.VMEM((blocks, 2 * ROWS, LANES), bf16),
            pltpu.VMEM((seq_count, 2 * ROWS, LANES), bf16),
            pltpu.VMEM((blocks, 2 * req_count, LANES), bf16),
            pltpu.VMEM((blocks, 2 * req_count, LANES), bf16),
            pltpu.VMEM((tp_count, req_count, out_cols), f32),
            pltpu.VMEM((tp_count, req_count, out_cols), f32),
            dma((4 * chunks + 1,)),
            dma((chunks, seq_count)),
            dma((chunks, seq_count)),
            dma((seq_count,)),
            dma((seq_count,)),
            dma((blocks,)),
            dma((blocks,)),
            dma((tp_count,)),
            dma((tp_count,)),
            dma((11,)),
        ],
        compiler_params=pltpu.CompilerParams(
            collective_id=0, has_side_effects=True, vmem_limit_bytes=64 * 1024 * 1024
        ),
        cost_estimate=pl.CostEstimate(
            flops=4 * 32 * cells * heads * DV + 2 * req_count * out_weight.size,
            bytes_accessed=4 * (key_pool.size + long_key.size) + 2 * out_weight.size,
            transcendentals=32 * cells * heads,
        ),
        name="decode",
    )(
        serve_table,
        serve_len,
        page_slot,
        page_offset,
        long_request,
        long_len,
        lambda_head,
        query,
        new_key,
        new_value,
        norm_gain.reshape(1, -1),
        key_pool,
        value_pool,
        long_key,
        long_value,
        out_weight,
    )


def solution(mesh):
    return jax.shard_map(
        functools.partial(on_device, mesh.shape["seq"], mesh.shape["tp"]),
        mesh=mesh,
        in_specs=(
            P("seq", "tp"),
            P("seq", "tp"),
            P("seq", "tp"),
            P("seq", None, "tp"),
            P("seq", None, "tp"),
            P(None, "seq", "tp"),
            P(None, "seq", "tp"),
            P("seq"),
            P("seq"),
            P("seq"),
            P("seq"),
            P(),
            P(),
            P("tp"),
            P("tp"),
            P("tp", None),
        ),
        out_specs=P("seq", "tp"),
        check_vma=False,
    )
```

```python
import functools

import jax
import jax.numpy as jnp
from jax import lax
from jax.experimental import pallas as pl
from jax.experimental.pallas import tpu as pltpu
from jax.sharding import PartitionSpec as P

DH = 128
DV = 256
PG = 64
LANES = 128
ROWS = 16
MASKED = -1e30
MESH = pl.DeviceIdType.MESH


def split3(x):
    high = x.astype(jnp.bfloat16).astype(jnp.float32)
    rest = x - high
    mid = rest.astype(jnp.bfloat16).astype(jnp.float32)
    return high, mid, rest - mid


def lane_pack(lane, columns):
    packed = jnp.zeros(lane.shape, jnp.float32)
    for at, column in enumerate(columns):
        packed = jnp.where(lane == at, column, packed)
    return packed


def kernel(
    seq_count,
    tp_count,
    heads,
    table_hbm,
    len_hbm,
    slot_hbm,
    offset_hbm,
    long_request_hbm,
    long_len_hbm,
    lambda_hbm,
    query_hbm,
    new_key_hbm,
    new_value_hbm,
    gain_hbm,
    key_ref,
    value_ref,
    long_key_ref,
    long_value_ref,
    weight_ref,
    out_ref,
    table_ref,
    len_ref,
    slot_ref,
    offset_ref,
    long_request_ref,
    long_len_ref,
    lambda_ref,
    query_ref,
    new_key_ref,
    new_value_ref,
    gain_ref,
    key_buf,
    value_buf,
    long_key_buf,
    long_value_buf,
    weight_buf,
    bias_buf,
    own_query,
    all_query,
    term_out,
    term_in,
    attn_out,
    attn_in,
    part_out,
    part_in,
    load_sem,
    query_send,
    query_recv,
    term_send,
    term_recv,
    attn_send,
    attn_recv,
    part_send,
    part_recv,
    small_sem,
):
    me = lax.axis_index("seq")
    tp_me = lax.axis_index("tp")
    blocks = heads * 2 * DV // LANES
    group = me // blocks
    block_me = me % blocks
    req_count = query_ref.shape[0]
    serve_count = table_ref.shape[0]
    page_count = slot_ref.shape[0]
    long_count = long_request_ref.shape[0]
    long_cells = long_key_ref.shape[1]
    pool_cells = page_count * PG
    out_cols = weight_ref.shape[1] // tp_count
    chunks = own_query.shape[0]
    chunk_heads = heads // chunks
    chunk_blocks = blocks // chunks
    width = chunk_heads * DV

    loads = []
    for h in range(chunks):
        cols = pl.ds(h * width, width)
        row = []
        for at, (src, dst) in enumerate(
            (
                (key_ref, key_buf),
                (long_key_ref, long_key_buf),
                (value_ref, value_buf),
                (long_value_ref, long_value_buf),
            )
        ):
            row.append(
                pltpu.make_async_copy(src.at[:, :, cols], dst.at[h], load_sem.at[4 * h + at])
            )
        loads.append(row)
    weight_load = pltpu.make_async_copy(weight_ref, weight_buf, load_sem.at[4 * chunks])

    smalls = [
        pltpu.make_async_copy(src, dst, small_sem.at[at])
        for at, (src, dst) in enumerate(
            (
                (query_hbm, query_ref),
                (table_hbm, table_ref),
                (len_hbm, len_ref),
                (slot_hbm, slot_ref),
                (offset_hbm, offset_ref),
                (long_request_hbm, long_request_ref),
                (long_len_hbm, long_len_ref),
                (new_key_hbm, new_key_ref),
                (lambda_hbm, lambda_ref),
                (new_value_hbm, new_value_ref),
                (gain_hbm, gain_ref),
            )
        )
    ]
    smalls[0].start()
    barrier = pltpu.get_barrier_semaphore()
    for k in range(1, seq_count):
        pl.semaphore_signal(
            barrier, inc=1, device_id={"seq": lax.rem(me + k, seq_count)}, device_id_type=MESH
        )
    for k in range(1, tp_count):
        pl.semaphore_signal(
            barrier, inc=1, device_id={"tp": lax.rem(tp_me + k, tp_count)}, device_id_type=MESH
        )
    for copy in smalls[1:]:
        copy.start()
    for copy in loads[0]:
        copy.start()
    smalls[0].wait()

    query = query_ref[...].astype(jnp.float32)
    half = width // 2
    for p in range(chunks):
        at = p * width
        packed = jnp.concatenate(
            [query[:, at : at + half], query[:, at + half : at + width]], axis=0
        ).astype(jnp.bfloat16)
        own_query[p] = packed
        all_query[p, me] = packed
    pl.semaphore_wait(barrier, seq_count + tp_count - 2)

    def query_copy(p, target, owner, at):
        return pltpu.make_async_remote_copy(
            src_ref=own_query.at[p],
            dst_ref=all_query.at[p, owner],
            send_sem=query_send.at[p, at],
            recv_sem=query_recv.at[p, owner],
            device_id={"seq": target},
            device_id_type=MESH,
        )

    for p in range(chunks):
        for k in range(1, seq_count):
            query_copy(p, lax.rem(me + k, seq_count), me, k - 1).start()
        if p + 1 < chunks:
            for copy in loads[p + 1]:
                copy.start()

    weight_load.start()
    for copy in smalls[1:]:
        copy.wait()

    lane = lax.broadcasted_iota(jnp.int32, (ROWS, LANES), 1)
    slot_row = lax.broadcasted_iota(jnp.int32, (ROWS, LANES), 0)
    length = jnp.zeros((ROWS, LANES), jnp.int32)
    owner = jnp.full((ROWS, LANES), -1, jnp.int32)
    for s in range(serve_count):
        length = jnp.where(slot_row == s, len_ref[s], length)
        owner = jnp.where(slot_row == s, table_ref[s], owner)
    for n in range(long_count):
        owner = jnp.where(slot_row == serve_count + n, long_request_ref[n], owner)
    per_chunk = LANES // PG
    for chunk in range(pool_cells // LANES):
        slot = jnp.full((ROWS, LANES), slot_ref[chunk * per_chunk], jnp.int32)
        offset = jnp.full((ROWS, LANES), offset_ref[chunk * per_chunk], jnp.int32)
        for extra in range(1, per_chunk):
            beyond = lane >= extra * PG
            slot = jnp.where(beyond, slot_ref[chunk * per_chunk + extra], slot)
            offset = jnp.where(beyond, offset_ref[chunk * per_chunk + extra], offset)
        live = (slot == slot_row) & (offset + (lane & (PG - 1)) < length)
        bias_buf[:, chunk * LANES : (chunk + 1) * LANES] = jnp.where(live, 0.0, MASKED)
    for n in range(long_count):
        for chunk in range(long_cells // LANES):
            pos = me * long_cells + chunk * LANES + lane
            live = (slot_row == serve_count + n) & (pos < long_len_ref[n])
            start = pool_cells + n * long_cells + chunk * LANES
            bias_buf[:, start : start + LANES] = jnp.where(live, 0.0, MASKED)

    products = query * new_key_ref[...].astype(jnp.float32)
    own_scores = [
        jnp.sum(products[:, m * DH : (m + 1) * DH], axis=1, keepdims=True) * DH ** (-0.5)
        for m in range(2 * heads)
    ]

    column = lax.broadcasted_iota(jnp.int32, (ROWS, seq_count * ROWS), 1)
    owner_wide = owner[:, :1]
    picks = []
    for part in range(2):
        local = (column & (ROWS - 1)) - part * req_count
        request = (column >> 4) * req_count + local
        hit = (local >= 0) & (local < req_count) & (request == owner_wide)
        picks.append(jnp.where(hit, 1.0, 0.0).astype(jnp.bfloat16))

    code = owner + 1
    id_high = (code >> 4).astype(jnp.float32)
    id_low = (code & 15).astype(jnp.float32)

    def term_copy(block, target, source):
        return pltpu.make_async_remote_copy(
            src_ref=term_out.at[block],
            dst_ref=term_in.at[source],
            send_sem=term_send.at[target],
            recv_sem=term_recv.at[source],
            device_id={"seq": target},
            device_id_type=MESH,
        )

    contract_last = (((1,), (1,)), ((), ()))
    for h in range(heads):
        p, inner = h // chunk_heads, h % chunk_heads
        lanes = slice(inner * DV, (inner + 1) * DV)
        if inner == 0:
            for copy in loads[p]:
                copy.wait()
            for k in range(1, seq_count):
                source = lax.rem(me + seq_count - k, seq_count)
                query_copy(p, me, source, k - 1).wait_recv()
            gathered = all_query[p].reshape(seq_count * ROWS, half)
            slot_query = jnp.concatenate(
                [jnp.dot(pick, gathered, preferred_element_type=jnp.float32) for pick in picks],
                axis=1,
            )
        maps = slot_query[:, lanes]
        blank = jnp.zeros((ROWS, DH), jnp.float32)
        spread = jnp.concatenate(
            [
                jnp.concatenate([maps[:, :DH], blank], axis=1),
                jnp.concatenate([blank, maps[:, DH:]], axis=1),
            ],
            axis=0,
        ).astype(jnp.bfloat16)
        pool_scores = lax.dot_general(
            spread,
            key_buf[p, :, :, lanes].reshape(pool_cells, 2 * DH),
            contract_last,
            preferred_element_type=jnp.float32,
        )
        long_scores = lax.dot_general(
            spread,
            long_key_buf[p, :, :, lanes].reshape(long_count * long_cells, 2 * DH),
            contract_last,
            preferred_element_type=jnp.float32,
        )
        bias = bias_buf[...]
        bias = jnp.concatenate([bias, bias], axis=0)
        pool_scores = pool_scores * DH ** (-0.5) + bias[:, :pool_cells]
        long_scores = long_scores * DH ** (-0.5) + bias[:, pool_cells:]
        best = jnp.maximum(
            jnp.max(pool_scores, axis=1, keepdims=True),
            jnp.max(long_scores, axis=1, keepdims=True),
        )
        pool_w = jnp.exp(pool_scores - best)
        long_w = jnp.exp(long_scores - best)
        total = jnp.sum(pool_w, axis=1, keepdims=True) + jnp.sum(long_w, axis=1, keepdims=True)
        numer = jnp.dot(
            pool_w.astype(jnp.bfloat16),
            value_buf[p, :, :, lanes].reshape(pool_cells, DV),
            preferred_element_type=jnp.float32,
        ) + jnp.dot(
            long_w.astype(jnp.bfloat16),
            long_value_buf[p, :, :, lanes].reshape(long_count * long_cells, DV),
            preferred_element_type=jnp.float32,
        )
        some = best > 0.5 * MASKED
        mean = jnp.where(some, numer / total, 0.0)
        level = jnp.where(some, best + jnp.log(total), MASKED)
        for j in range(2):
            rows = slice(j * ROWS, (j + 1) * ROWS)
            meta = lane_pack(lane, (*split3(level[rows]), id_high, id_low))
            for c in range(2):
                block = (h * 2 + j) * 2 + c
                term_out[block] = jnp.concatenate(
                    [mean[rows, c * LANES : (c + 1) * LANES], meta], axis=0
                ).astype(jnp.bfloat16)
        if inner == chunk_heads - 1:
            for g in range(seq_count // blocks):
                for k in range(chunk_blocks):
                    block = p * chunk_blocks + lax.rem(me + k, chunk_blocks)
                    target = g * blocks + block
                    if k:
                        term_copy(block, target, me).start()
                    else:

                        @pl.when(target != me)
                        def _():
                            term_copy(block, target, me).start()

    term_in[me] = term_out[block_me]
    for k in range(1, seq_count):
        source = lax.rem(me + seq_count - k, seq_count)
        term_copy(0, me, source).wait_recv()

    terms = term_in[...]
    means = terms[:, :ROWS].reshape(seq_count * ROWS, LANES)
    meta = jnp.transpose(terms[:, ROWS:].reshape(seq_count * ROWS, LANES).astype(jnp.float32))
    level = (meta[2:3] + meta[1:2]) + meta[0:1]
    ids = (meta[3:4] * 16.0 + meta[4:5]).astype(jnp.int32) - 1
    handled = blocks * req_count
    request = group * handled + lax.broadcasted_iota(
        jnp.int32, (handled, seq_count * ROWS), 0
    )
    member = request == ids
    top = jnp.max(jnp.where(member, level, MASKED), axis=1, keepdims=True)
    factor = jnp.where(member, jnp.exp(jnp.where(member, level - top, 0.0)), 0.0)
    total = jnp.sum(factor, axis=1, keepdims=True)
    high = factor.astype(jnp.bfloat16)
    low = (factor - high.astype(jnp.float32)).astype(jnp.bfloat16)
    merged = jnp.dot(high, means, preferred_element_type=jnp.float32) + jnp.dot(
        low, means, preferred_element_type=jnp.float32
    )
    some = total > 0.0
    safe = jnp.where(some, total, 1.0)
    merged = merged / safe
    level = jnp.where(some, top + jnp.log(safe), MASKED)
    wide = lax.broadcasted_iota(jnp.int32, (handled, LANES), 1)
    meta = lane_pack(wide, split3(level))
    attn_out[...] = jnp.concatenate(
        [
            merged.reshape(blocks, req_count, LANES),
            meta.reshape(blocks, req_count, LANES),
        ],
        axis=1,
    ).astype(jnp.bfloat16)

    def attn_copy(home, source_block):
        return pltpu.make_async_remote_copy(
            src_ref=attn_out.at[home],
            dst_ref=attn_in.at[source_block],
            send_sem=attn_send.at[home],
            recv_sem=attn_recv.at[source_block],
            device_id={"seq": group * blocks + home},
            device_id_type=MESH,
        )

    for k in range(1, blocks):
        attn_copy(lax.rem(block_me + k, blocks), block_me).start()
    attn_in[block_me] = attn_out[block_me]
    weight_load.wait()
    for k in range(1, blocks):
        attn_copy(block_me, lax.rem(block_me + blocks - k, blocks)).wait_recv()

    value = new_value_ref[...].astype(jnp.float32)
    normed = []
    for h in range(heads):
        diffs = []
        for c in range(2):
            attn = []
            for j in range(2):
                got = attn_in[(h * 2 + j) * 2 + c].astype(jnp.float32)
                info = got[req_count:]
                level = (info[:, 2:3] + info[:, 1:2]) + info[:, 0:1]
                score = own_scores[2 * h + j]
                top = jnp.maximum(score, level)
                own_w = jnp.exp(score - top)
                kept_w = jnp.exp(level - top)
                at = h * DV + c * LANES
                attn.append(
                    (own_w * value[:, at : at + LANES] + kept_w * got[:req_count])
                    / (own_w + kept_w)
                )
            diffs.append(attn[0] - lambda_ref[h] * attn[1])
        diff = jnp.concatenate(diffs, axis=1)
        square = jnp.sum(diff * diff, axis=1, keepdims=True) * (1.0 / DV)
        normed.append(
            diff * lax.rsqrt(square + 1e-05) * gain_ref[:, h * DV : (h + 1) * DV]
        )
    normed = jnp.concatenate(normed, axis=1).astype(jnp.bfloat16)

    def part_copy(target, source):
        return pltpu.make_async_remote_copy(
            src_ref=part_out.at[target],
            dst_ref=part_in.at[source],
            send_sem=part_send.at[target],
            recv_sem=part_recv.at[source],
            device_id={"tp": target},
            device_id_type=MESH,
        )

    def partial_out(target):
        cols = pl.ds(pl.multiple_of(target * out_cols, LANES), out_cols)
        return jnp.dot(normed, weight_buf[:, cols], preferred_element_type=jnp.float32)

    for k in range(1, tp_count):
        target = lax.rem(tp_me + k, tp_count)
        part_out[target] = partial_out(target)
        part_copy(target, tp_me).start()
    result = partial_out(tp_me)
    for k in range(1, tp_count):
        source = lax.rem(tp_me + tp_count - k, tp_count)
        part_copy(tp_me, source).wait_recv()
        result = result + part_in[source]
    out_ref[...] = result.astype(jnp.bfloat16)

    for k in range(1, seq_count):
        for p in range(chunks):
            query_copy(p, lax.rem(me + k, seq_count), me, k - 1).wait_send()
        term_copy(0, lax.rem(me + k, seq_count), me).wait_send()
    for k in range(1, blocks):
        attn_copy(lax.rem(block_me + k, blocks), block_me).wait_send()
    for k in range(1, tp_count):
        part_copy(lax.rem(tp_me + k, tp_count), tp_me).wait_send()


def on_device(
    seq_count,
    tp_count,
    query,
    new_key,
    new_value,
    key_pool,
    value_pool,
    long_key,
    long_value,
    serve_table,
    serve_len,
    page_slot,
    page_offset,
    long_request,
    long_len,
    lambda_head,
    norm_gain,
    out_weight,
):
    heads = lambda_head.shape[0]
    req_count = query.shape[0]
    blocks = heads * 2 * DV // LANES
    pages = key_pool.shape[0]
    long_count, long_cells = long_key.shape[:2]
    out_cols = out_weight.shape[1] // tp_count
    chunks = heads
    width = heads // chunks * DV
    cells = pages * PG + long_count * long_cells
    vmem = pl.BlockSpec(memory_space=pltpu.VMEM)
    hbm = pl.BlockSpec(memory_space=pl.ANY)
    bf16, f32 = jnp.bfloat16, jnp.float32
    dma = pltpu.SemaphoreType.DMA
    return pl.pallas_call(
        functools.partial(kernel, seq_count, tp_count, heads),
        out_shape=jax.ShapeDtypeStruct((req_count, out_cols), bf16),
        in_specs=[hbm] * 16,
        out_specs=vmem,
        scratch_shapes=[
            pltpu.SMEM(serve_table.shape, jnp.int32),
            pltpu.SMEM(serve_len.shape, jnp.int32),
            pltpu.SMEM(page_slot.shape, jnp.int32),
            pltpu.SMEM(page_offset.shape, jnp.int32),
            pltpu.SMEM(long_request.shape, jnp.int32),
            pltpu.SMEM(long_len.shape, jnp.int32),
            pltpu.SMEM(lambda_head.shape, f32),
            pltpu.VMEM(query.shape, bf16),
            pltpu.VMEM(new_key.shape, bf16),
            pltpu.VMEM(new_value.shape, bf16),
            pltpu.VMEM((1, norm_gain.size), f32),
            pltpu.VMEM((chunks, pages, PG, width), bf16),
            pltpu.VMEM((chunks, pages, PG, width), bf16),
            pltpu.VMEM((chunks, long_count, long_cells, width), bf16),
            pltpu.VMEM((chunks, long_count, long_cells, width), bf16),
            pltpu.VMEM(out_weight.shape, bf16),
            pltpu.VMEM((ROWS, cells), f32),
            pltpu.VMEM((chunks, 2 * req_count, width // 2), bf16),
            pltpu.VMEM((chunks, seq_count, 2 * req_count, width // 2), bf16),
            pltpu.VMEM((blocks, 2 * ROWS, LANES), bf16),
            pltpu.VMEM((seq_count, 2 * ROWS, LANES), bf16),
            pltpu.VMEM((blocks, 2 * req_count, LANES), bf16),
            pltpu.VMEM((blocks, 2 * req_count, LANES), bf16),
            pltpu.VMEM((tp_count, req_count, out_cols), f32),
            pltpu.VMEM((tp_count, req_count, out_cols), f32),
            dma((4 * chunks + 1,)),
            dma((chunks, seq_count)),
            dma((chunks, seq_count)),
            dma((seq_count,)),
            dma((seq_count,)),
            dma((blocks,)),
            dma((blocks,)),
            dma((tp_count,)),
            dma((tp_count,)),
            dma((11,)),
        ],
        compiler_params=pltpu.CompilerParams(
            collective_id=0, has_side_effects=True, vmem_limit_bytes=64 * 1024 * 1024
        ),
        cost_estimate=pl.CostEstimate(
            flops=4 * 32 * cells * heads * DV + 2 * req_count * out_weight.size,
            bytes_accessed=4 * (key_pool.size + long_key.size) + 2 * out_weight.size,
            transcendentals=32 * cells * heads,
        ),
        name="decode",
    )(
        serve_table,
        serve_len,
        page_slot,
        page_offset,
        long_request,
        long_len,
        lambda_head,
        query,
        new_key,
        new_value,
        norm_gain.reshape(1, -1),
        key_pool,
        value_pool,
        long_key,
        long_value,
        out_weight,
    )


def solution(mesh):
    return jax.shard_map(
        functools.partial(on_device, mesh.shape["seq"], mesh.shape["tp"]),
        mesh=mesh,
        in_specs=(
            P("seq", "tp"),
            P("seq", "tp"),
            P("seq", "tp"),
            P("seq", None, "tp"),
            P("seq", None, "tp"),
            P(None, "seq", "tp"),
            P(None, "seq", "tp"),
            P("seq"),
            P("seq"),
            P("seq"),
            P("seq"),
            P(),
            P(),
            P("tp"),
            P("tp"),
            P("tp", None),
        ),
        out_specs=P("seq", "tp"),
        check_vma=False,
    )
```
